256 devices in a mesh: row: 16 (over z, x_lo), col: 16 (over x_hi, y, core).
Axes of the slice: x: 4 (x_hi: 2, x_lo: 2; x = x_hi * 2 + x_lo), y: 4, z: 8, core: 2. Of those that a mesh axis runs over, the one named last changes fastest.
Arguments:
- replica_weights: float32 [16, 16, 128, 2048], P('row', 'col'), may hold values from -4.5 to 4.5
- replica_first: float32 [16, 16, 128, 2048], P('row', 'col'), may hold values from -3.9 to 3.9
- replica_second: float32 [16, 16, 128, 2048], P('row', 'col'), may hold values from 0.05 to 8
- replica_grads: float32 [16, 16, 128, 2048], P('row', 'col'), may hold values from -9 to 9
Outputs:
- mean_weights: float32 [128, 2048], replicated
- mean_first: float32 [128, 2048], replicated
- mean_second: float32 [128, 2048], replicated
The draws below stay inside these ranges and needn't reach their ends.
All inputs are finite; a program needn't handle non-finite values.
Results may differ from the reference program's by a relative error of at most 0.00002.
Values sent between devices are 32-bit elements; how exact they have to be, the bound alone decides.
No kernel may reach another device: no remote copies, remote signals or barrier semaphores. Data moves between devices by JAX's collectives and lax.ppermute only.
A program may use at most 64 MiB of HBM per device.

```python
import jax
import jax.numpy as jnp
from jax import lax

D = 2048
WROWS = 128
N_ROW = 16
N_COL = 16


def signed_field(key, spread, salt):
    base = jax.random.truncated_normal(jax.random.fold_in(key, salt), -3.0, 3.0, (WROWS, D), jnp.float32)
    jitter = jax.random.truncated_normal(jax.random.fold_in(key, salt + 1), -3.0, 3.0, (N_ROW, N_COL, WROWS, D), jnp.float32)
    return base[None, None] + spread * jitter


def draw_replica_weights(key, part):
    return signed_field(key, 0.5, 11)


def draw_replica_first(key, part):
    return signed_field(key, 0.3, 21)


def draw_replica_grads(key, part):
    return 2.0 * signed_field(key, 0.5, 31)


def draw_replica_second(key, part):
    base = jnp.exp(jax.random.uniform(jax.random.fold_in(key, 41), (WROWS, D), jnp.float32, jnp.log(0.1), jnp.log(4.0)))
    factor = jnp.exp(jax.random.uniform(jax.random.fold_in(key, 42), (N_ROW, N_COL, WROWS, D), jnp.float32, jnp.log(0.5), jnp.log(2.0)))
    return base[None, None] * factor


def setup_inputs(seed: int = 0) -> dict:
    key_list = jax.random.split(jax.random.key(seed), 5)
    return {
        "replica_weights": draw_replica_weights(jax.random.fold_in(key_list[4], 71), 0),
        "replica_first": draw_replica_first(jax.random.fold_in(key_list[4], 71), 0),
        "replica_second": draw_replica_second(jax.random.fold_in(key_list[4], 71), 0),
        "replica_grads": draw_replica_grads(jax.random.fold_in(key_list[4], 71), 0),
    }


bias_one = 0.9999734386011124
bias_two = 0.994079470779666

def reference(replica_weights, replica_first, replica_second, replica_grads):
    first = 0.9 * replica_first + 0.1 * replica_grads
    second = 0.95 * replica_second + 0.05 * replica_grads * replica_grads
    update = first / bias_one / (jnp.sqrt(second / bias_two) + 1e-08) + 0.1 * replica_weights
    weights = replica_weights - 0.003 * update
    return (lax.optimization_barrier(jnp.mean(weights, axis=(0, 1))), lax.optimization_barrier(jnp.mean(first, axis=(0, 1))), lax.optimization_barrier(jnp.mean(second, axis=(0, 1))))
```

```python
import jax
import jax.numpy as jnp
from jax import lax
from jax.experimental import pallas as pl
from jax.experimental.pallas import tpu as pltpu
from jax.sharding import Mesh, PartitionSpec as P

bias_one = 0.9999734386011124
bias_two = 0.994079470779666

PARTS = (("zh", 2), ("zm", 2), ("zl", 2), ("xl", 2), ("xh", 2), ("y", 4), ("c", 2))
NEAR = ("zl", "xh", "xl", "y")
PEERS = 32
ROWS, D = 128, 2048
HALF = ROWS // 2
WIDE = D // 4
STEPS = 4
STEP_ROWS = HALF // STEPS
STEP_PEERS = PEERS // STEPS


def adam_kernel(half, weights_ref, first_ref, second_ref, grads_ref, out_ref):
    gradient = grads_ref[0, 0]
    old = weights_ref[0, 0]
    first = 0.9 * first_ref[0, 0] + 0.1 * gradient
    second = 0.95 * second_ref[0, 0] + 0.05 * gradient * gradient
    bottom = bias_one * jnp.sqrt(second * (1.0 / bias_two)) + bias_one * 1e-08
    weights = old - 0.003 * (first / bottom + 0.1 * old)
    for k, value in enumerate((weights, first, second)):
        for p in range(STEP_PEERS):
            r, g = p // 4, p % 4
            out_ref[p, :, k * WIDE : (k + 1) * WIDE] = value[8 * r : 8 * r + 8, g * WIDE : (g + 1) * WIDE]


def adam_half(half, weights, first, second, grads):
    block = pl.BlockSpec((1, 1, STEP_ROWS, D), lambda i, half: (0, 0, half[0] * STEPS + i, 0))
    return pl.pallas_call(
        adam_kernel,
        grid_spec=pltpu.PrefetchScalarGridSpec(
            num_scalar_prefetch=1,
            grid=(STEPS,),
            in_specs=[block] * 4,
            out_specs=pl.BlockSpec((STEP_PEERS, 8, 3 * WIDE), lambda i, half: (i, 0, 0)),
        ),
        out_shape=jax.ShapeDtypeStruct((PEERS, 8, 3 * WIDE), jnp.float32),
        cost_estimate=pl.CostEstimate(flops=30 * HALF * D, bytes_accessed=28 * HALF * D, transcendentals=2 * HALF * D),
        name="adam_half",
    )(half, weights, first, second, grads)


def place_kernel(half, data_ref, *refs):
    outs = refs[-3:]
    for k in range(3):
        for p in range(STEP_PEERS):
            r, g = p // 4, p % 4
            outs[k][8 * r : 8 * r + 8, g * WIDE : (g + 1) * WIDE] = data_ref[p, :, k * WIDE : (k + 1) * WIDE]


def place_half(half, data, before=()):
    return pl.pallas_call(
        place_kernel,
        grid_spec=pltpu.PrefetchScalarGridSpec(
            num_scalar_prefetch=1,
            grid=(STEPS,),
            in_specs=[pl.BlockSpec((STEP_PEERS, 8, 3 * WIDE), lambda i, half: (i, 0, 0))]
            + [pl.BlockSpec(memory_space=pl.ANY)] * len(before),
            out_specs=[pl.BlockSpec((STEP_ROWS, D), lambda i, half: (half[0] * STEPS + i, 0))] * 3,
        ),
        out_shape=[jax.ShapeDtypeStruct((ROWS, D), jnp.float32)] * 3,
        input_output_aliases={2 + k: k for k in range(len(before))},
        cost_estimate=pl.CostEstimate(flops=0, bytes_accessed=24 * HALF * D, transcendentals=0),
        name="place_half",
    )(half, data, *before)


def across_cores(x):
    return lax.ppermute(x, "c", [(0, 1), (1, 0)])


FAR = "ppermute3"


def far_sum(x):
    if FAR == "ppermute2":
        x = x + lax.ppermute(x, "zm", [(0, 1), (1, 0)])
        return x + lax.ppermute(x, "zh", [(0, 1), (1, 0)])
    if FAR == "ppermute3":
        axes = ("zh", "zm")
        other = [lax.ppermute(x, axes, [(i, (i + d) % 4) for i in range(4)]) for d in (1, 3, 2)]
        return (x + other[2]) + (other[0] + other[1])
    y = lax.all_to_all(jnp.broadcast_to(x[None], (4,) + x.shape), ("zh", "zm"), 0, 0, tiled=True)
    return (y[0] + y[1]) + (y[2] + y[3])


def on_device(*arrays):
    core = lax.axis_index("c").astype(jnp.int32).reshape(1)
    theirs = adam_half(1 - core, *arrays)
    received = across_cores(theirs)
    mine = adam_half(core, *arrays)
    mine = mine + received
    pieces = lax.all_to_all(mine, NEAR, 0, 0, tiled=True)
    piece = far_sum(jnp.sum(pieces, axis=0)) * (1.0 / 256.0)
    mine = lax.all_to_all(jnp.broadcast_to(piece[None], (PEERS,) + piece.shape), NEAR, 0, 0, tiled=True)
    theirs = across_cores(mine)
    outs = place_half(core, mine)
    return tuple(place_half(1 - core, theirs, outs))


def solution(mesh):
    names, sizes = zip(*PARTS)
    parts = Mesh(mesh.devices.reshape(sizes), names)
    spec = P(("zh", "zm", "zl", "xl"), ("xh", "y", "c"), None, None)
    return jax.shard_map(on_device, mesh=parts, in_specs=(spec,) * 4, out_specs=(P(),) * 3, check_vma=False)
```

```python
import jax
import jax.numpy as jnp
from jax import lax
from jax.experimental import pallas as pl
from jax.experimental.pallas import tpu as pltpu
from jax.sharding import PartitionSpec as P

bias_one = 0.9999734386011124
bias_two = 0.994079470779666

AXES = ("row", "col")
SHIFT = (0, 0)


def device(x, y, z, core):
    return (z % 8 * 2 + x % 2) * 16 + x // 2 * 8 + y * 2 + core


def place(core, along, pair, across, far):
    x, y = (along, across) if core == 0 else (across, along)
    return device(x, y, 2 * far + pair + SHIFT[core], core)


def ring(change):
    return [
        (place(core, along, pair, across, far), place(core, (along + change) % 4, pair, across, far))
        for core in range(2) for along in range(4) for pair in range(2) for across in range(4) for far in range(4)
    ]


SECOND = [
    [place(core, along, pair, across, far) for across in range(4) for pair in range(2)]
    for core in range(2) for along in range(4) for far in range(4)
]


def far_pairs(change):
    return [
        (device(x, y, 2 * far + pair + SHIFT[core], core), device(x, y, 2 * change(far) + pair + SHIFT[core], core))
        for core in range(2) for far in range(4) for pair in range(2) for x in range(4) for y in range(4)
    ]


PEERS = 32
ROWS, D = 128, 2048
HALF = ROWS // 2
WIDE = D // 4
STEPS = 4
ROOM_A = 60 << 20
ROOM_B = 8 << 20
VMEM = 8 << 20
STEP_ROWS = HALF // STEPS
STEP_PEERS = PEERS // STEPS


def place_kernel(rows, *refs):
    outs, sems = refs[-4:-1], refs[-1]
    copies = [
        pltpu.make_async_copy(
            refs[i].at[:, g, :, pl.ds(k * WIDE, WIDE)],
            outs[k].at[pl.ds(rows[i], 2), :, pl.ds(g * WIDE, WIDE)],
            sems.at[i, k, g],
        )
        for i in range(sems.shape[0])
        for k in range(3)
        for g in range(4)
    ]
    for copy in copies:
        copy.start()
    for copy in copies:
        copy.wait()


def place_chunks(rows, chunks, before):
    anywhere = pl.BlockSpec(memory_space=pl.ANY)
    n = len(chunks)
    return pl.pallas_call(
        place_kernel,
        in_specs=[pl.BlockSpec(memory_space=pltpu.SMEM)] + [anywhere] * (n + len(before)),
        out_specs=[anywhere] * 3,
        out_shape=[jax.ShapeDtypeStruct((ROWS // 8, 8, D), jnp.float32)] * 3,
        scratch_shapes=[pltpu.SemaphoreType.DMA((n, 3, 4))],
        input_output_aliases={1 + n + k: k for k in range(len(before))},
        compiler_params=pltpu.CompilerParams(vmem_limit_bytes=8 << 20),
        cost_estimate=pl.CostEstimate(flops=0, bytes_accessed=n * 24 * 16 * D, transcendentals=0),
        name="place_chunks",
    )(jnp.stack(rows).astype(jnp.int32), *(chunk.reshape(2, 4, 8, 3 * WIDE) for chunk in chunks), *before)


def across_cores(x):
    return lax.ppermute(x, AXES, [(i, i ^ 1) for i in range(256)])


def exchange(x, groups):
    return lax.all_to_all(x, AXES, 0, 0, axis_index_groups=groups, tiled=True)


def repeat(x, groups):
    return jnp.broadcast_to(x[None], (len(groups[0]),) + x.shape)


def far_sum(x):
    x = x + lax.ppermute(x, AXES, far_pairs(lambda far: far ^ 1))
    return x + lax.ppermute(x, AXES, far_pairs(lambda far: far ^ 3))


def adam(half, arrays):
    old, first, second, gradient = (lax.dynamic_slice_in_dim(x[0, 0], half * HALF, HALF, 0) for x in arrays)
    first = 0.9 * first + 0.1 * gradient
    second = 0.95 * second + 0.05 * gradient * gradient
    bottom = bias_one * jnp.sqrt(second * (1.0 / bias_two)) + bias_one * 1e-08
    return old - 0.003 * (first / bottom + 0.1 * old), first, second


def join_kernel(at, *refs):
    for d in range(4):

        @pl.when(pl.program_id(0) == d)
        def _():
            for k in range(3):
                for p in range(8):
                    part = (slice(8 * (p // 4), 8 * (p // 4) + 8), slice(p % 4 * WIDE, (p % 4 + 1) * WIDE))
                    refs[6 + d][p, :, k * WIDE : (k + 1) * WIDE] = refs[k][part] + refs[3 + k][part]


def join(at, mine, theirs):
    return pl.pallas_call(
        join_kernel,
        grid_spec=pltpu.PrefetchScalarGridSpec(
            num_scalar_prefetch=1,
            grid=(4,),
            in_specs=[pl.BlockSpec((16, D), lambda i, at: (lax.rem(at[0] + i, 4), 0))] * 6,
            out_specs=[pl.BlockSpec((8, 8, 3 * WIDE), lambda i, at: (0, 0, 0))] * 4,
        ),
        out_shape=[jax.ShapeDtypeStruct((8, 8, 3 * WIDE), jnp.float32)] * 4,
        compiler_params=pltpu.CompilerParams(vmem_limit_bytes=16 << 20),
        cost_estimate=pl.CostEstimate(flops=3 * HALF * D, bytes_accessed=36 * HALF * D, transcendentals=0),
        name="join",
    )(at, *mine, *theirs)


def on_device(*arrays):
    row, col = lax.axis_index("row").astype(jnp.int32), lax.axis_index("col").astype(jnp.int32)
    core = lax.rem(col, 2)
    x, y = col // 8 * 2 + lax.rem(row, 2), lax.rem(col // 2, 4)
    mine_at, their_at = jnp.where(core == 0, x, y), jnp.where(core == 0, y, x)
    sent = adam(1 - core, arrays)
    theirs = [across_cores(a) for a in sent]
    arrays, _ = lax.optimization_barrier((arrays, sent))
    chunks = join(mine_at.reshape(1), adam(core, arrays), theirs)
    other = [lax.ppermute(chunks[d], AXES, ring(d)) for d in (1, 2, 3)]
    mine = (chunks[0] + other[1]) + (other[0] + other[2])
    mine = jnp.sum(exchange(mine, SECOND), axis=0)
    mine = far_sum(mine) * (1.0 / 256.0)
    mine = exchange(repeat(mine, SECOND), SECOND)
    chunks = [mine] + [lax.ppermute(mine, AXES, ring(d)) for d in (1, 2, 3)]
    rows = [core * 8 + lax.rem(mine_at + 4 - d, 4) * 2 for d in range(4)]
    their_rows = [(1 - core) * 8 + lax.rem(their_at + 4 - d, 4) * 2 for d in range(4)]
    theirs, outs = [across_cores(chunks[0])], ()
    for d in range(1, 4):
        ready = [(rows[d - 1], chunks[d - 1])] + [(their_rows[d - 2], theirs[d - 2])] * (d >= 2)
        outs = place_chunks(*zip(*ready), outs)
        chunk, outs = lax.optimization_barrier((chunks[d], outs))
        theirs.append(across_cores(chunk))
        chunks[d] = chunk
    outs = place_chunks((rows[3], their_rows[2]), (chunks[3], theirs[2]), outs)
    outs = place_chunks((their_rows[3],), (theirs[3],), outs)
    return tuple(out.reshape(ROWS, D) for out in outs)


def solution(mesh):
    spec = P("row", "col", None, None)
    return jax.shard_map(on_device, mesh=mesh, in_specs=(spec,) * 4, out_specs=(P(),) * 3, check_vma=False)
```

```python
import functools

import jax
import jax.numpy as jnp
from jax import lax
from jax.experimental import pallas as pl
from jax.experimental.pallas import tpu as pltpu
from jax.sharding import PartitionSpec as P

bias_one = 0.9999734386011124
bias_two = 0.994079470779666

AXES = ("row", "col")
SHIFT = (0, 0)
WAYS = (2, 1, 3)


def device(x, y, z, core):
    return (z % 8 * 2 + x % 2) * 16 + x // 2 * 8 + y * 2 + core


def place(core, along, pair, across, far):
    x, y = (along, across) if core == 0 else (across, along)
    return device(x, y, 2 * far + pair + SHIFT[core], core)


def ring(change):
    return [
        (place(core, along, pair, across, far), place(core, (along + change) % 4, pair, across, far))
        for core in range(2) for along in range(4) for pair in range(2) for across in range(4) for far in range(4)
    ]


SECOND = [
    [place(core, along, pair, across, far) for across in range(4) for pair in range(2)]
    for core in range(2) for along in range(4) for far in range(4)
]


def far_pairs(change):
    return [
        (device(x, y, 2 * far + pair + SHIFT[core], core), device(x, y, 2 * change(far) + pair + SHIFT[core], core))
        for core in range(2) for far in range(4) for pair in range(2) for x in range(4) for y in range(4)
    ]


PEERS = 32
ROWS, D = 128, 2048
HALF = ROWS // 2
WIDE = D // 4
STEPS = 4
ROOM_A = 60 << 20
ROOM_B = 8 << 20
VMEM = 8 << 20
STEP_ROWS = HALF // STEPS
STEP_PEERS = PEERS // STEPS


def place_kernel(which, at, *refs):
    outs, sems = refs[-4:-1], refs[-1]
    copies = [
        pltpu.make_async_copy(
            refs[i].at[:, g, :, pl.ds(k * WIDE, WIDE)],
            outs[k].at[pl.ds(at[8 + which[i]], 2), :, pl.ds(g * WIDE, WIDE)],
            sems.at[i, k, g],
        )
        for i in range(sems.shape[0])
        for k in range(3)
        for g in range(4)
    ]
    for copy in copies:
        copy.start()
    for copy in copies:
        copy.wait()


def place_chunks(at, every, which, before):
    chunks = [every[i] for i in which]
    anywhere = pl.BlockSpec(memory_space=pl.ANY)
    n = len(chunks)
    return pl.pallas_call(
        functools.partial(place_kernel, which),
        in_specs=[pl.BlockSpec(memory_space=pltpu.SMEM)] + [anywhere] * (n + len(before)),
        out_specs=[anywhere] * 3,
        out_shape=[jax.ShapeDtypeStruct((ROWS // 8, 8, D), jnp.float32)] * 3,
        scratch_shapes=[pltpu.SemaphoreType.DMA((n, 3, 4))],
        input_output_aliases={1 + n + k: k for k in range(len(before))},
        compiler_params=pltpu.CompilerParams(vmem_limit_bytes=8 << 20),
        name="place_chunks",
    )(at, *(chunk.reshape(2, 4, 8, 3 * WIDE) for chunk in chunks), *before)


def across_cores(x):
    return lax.ppermute(x, AXES, [(i, i ^ 1) for i in range(256)])


def exchange(x, groups):
    return lax.all_to_all(x, AXES, 0, 0, axis_index_groups=groups, tiled=True)


def repeat(x, groups):
    return jnp.broadcast_to(x[None], (len(groups[0]),) + x.shape)


def far_sum(x):
    x = x + lax.ppermute(x, AXES, far_pairs(lambda far: far ^ 1))
    return x + lax.ppermute(x, AXES, far_pairs(lambda far: far ^ 3))


def adam(arrays):
    old, first, second, gradient = (x[0, 0] for x in arrays)
    first = 0.9 * first + 0.1 * gradient
    second = 0.95 * second + 0.05 * gradient * gradient
    scaled = second * (1.0 / bias_two)
    bottom = bias_one * (scaled * lax.rsqrt(scaled)) + bias_one * 1e-08
    return old - 0.003 * (first / bottom + 0.1 * old), first, second


def arrange(block, out_ref, added=None):
    for k in range(3):
        for p in range(8):
            value = block[k][8 * (p // 4) : 8 * (p // 4) + 8, p % 4 * WIDE : (p % 4 + 1) * WIDE]
            place = (p, slice(None), slice(k * WIDE, (k + 1) * WIDE))
            out_ref[place] = value if added is None else value + added[place]


def send_kernel(at, *refs):
    for i in range(len(refs) - 3):

        @pl.when(pl.program_id(0) == i)
        def _():
            arrange(refs[:3], refs[3 + i])


def join_kernel(at, weights, first, second, added, out):
    arrange((weights, first, second), out, added)


CHUNK = (8, 8, 3 * WIDE)


def send_chunks(at, arrays, order):
    steps = len(order)

    def source(i, at):
        where = at[4 + order[-1]]
        for n in range(steps - 1):
            where = jnp.where(i == n, at[4 + order[n]], where)
        return where, 0

    return pl.pallas_call(
        send_kernel,
        grid_spec=pltpu.PrefetchScalarGridSpec(
            num_scalar_prefetch=1,
            grid=(steps,),
            in_specs=[pl.BlockSpec((16, D), source)] * 3,
            out_specs=[pl.BlockSpec(CHUNK, lambda i, at: (0, 0, 0))] * steps,
        ),
        out_shape=[jax.ShapeDtypeStruct(CHUNK, jnp.float32)] * steps,
        compiler_params=pltpu.CompilerParams(vmem_limit_bytes=12 << 20),
        name="send_chunks",
    )(at, *arrays)


def join_chunk(at, arrays, received, d):
    return pl.pallas_call(
        join_kernel,
        grid_spec=pltpu.PrefetchScalarGridSpec(
            num_scalar_prefetch=1,
            grid=(1,),
            in_specs=[pl.BlockSpec((16, D), lambda i, at: (at[d], 0))] * 3 + [pl.BlockSpec(CHUNK, lambda i, at: (0, 0, 0))],
            out_specs=pl.BlockSpec(CHUNK, lambda i, at: (0, 0, 0)),
        ),
        out_shape=jax.ShapeDtypeStruct(CHUNK, jnp.float32),
        compiler_params=pltpu.CompilerParams(vmem_limit_bytes=8 << 20),
        name="join_chunk",
    )(at, *arrays, received)


def on_device(*arrays):
    row, col = lax.axis_index("row").astype(jnp.int32), lax.axis_index("col").astype(jnp.int32)
    core = lax.rem(col, 2)
    x, y = col // 8 * 2 + lax.rem(row, 2), lax.rem(col // 2, 4)
    mine_at, their_at = jnp.where(core == 0, x, y), jnp.where(core == 0, y, x)
    ahead = [core * 4 + lax.rem(mine_at + d, 4) for d in range(4)] + [(1 - core) * 4 + lax.rem(their_at + d, 4) for d in range(4)]
    behind = [core * 8 + lax.rem(mine_at + 4 - d, 4) * 2 for d in (0,) + WAYS]
    behind += [(1 - core) * 8 + lax.rem(their_at + 4 - d, 4) * 2 for d in (0,) + WAYS]
    at = jnp.stack(ahead + behind).astype(jnp.int32)
    arrays = adam(arrays)
    order = WAYS + (0,)
    received = [across_cores(chunk) for chunk in send_chunks(at, arrays, order)]
    sums = [join_chunk(at, arrays, theirs, d) for theirs, d in zip(received, order)]
    other = [lax.ppermute(chunk, AXES, ring(d)) for chunk, d in zip(sums, WAYS)]
    mine = (sums[3] + other[0]) + (other[1] + other[2])
    mine = jnp.sum(exchange(mine, SECOND), axis=0)
    mine = far_sum(mine) * (1.0 / 256.0)
    mine = exchange(repeat(mine, SECOND), SECOND)
    chunks = [mine] + [lax.ppermute(mine, AXES, ring(d)) for d in WAYS]
    chunks += [across_cores(chunk) for chunk in chunks]
    outs = place_chunks(at, chunks, (0, 1, 2, 3, 4, 5), ())
    outs = place_chunks(at, chunks, (6, 7), outs)
    return tuple(out.reshape(ROWS, D) for out in outs)


def solution(mesh):
    spec = P("row", "col", None, None)
    return jax.shard_map(on_device, mesh=mesh, in_specs=(spec,) * 4, out_specs=(P(),) * 3, check_vma=False)
```

```python
import functools

import jax
import jax.numpy as jnp
from jax import lax
from jax.experimental import pallas as pl
from jax.experimental.pallas import tpu as pltpu
from jax.sharding import PartitionSpec as P

bias_one = 0.9999734386011124
bias_two = 0.994079470779666

AXES = ("row", "col")
SHIFT = (0, 0)
WAYS = (2, 1, 3)
SPLIT = 6


def device(x, y, z, core):
    return (z % 8 * 2 + x % 2) * 16 + x // 2 * 8 + y * 2 + core


def place(core, along, pair, across, far):
    x, y = (along, across) if core == 0 else (across, along)
    return device(x, y, 2 * far + pair + SHIFT[core], core)


def ring(change):
    return [
        (place(core, along, pair, across, far), place(core, (along + change) % 4, pair, across, far))
        for core in range(2) for along in range(4) for pair in range(2) for across in range(4) for far in range(4)
    ]


SECOND = [
    [place(core, along, pair, across, far) for across in range(4) for pair in range(2)]
    for core in range(2) for along in range(4) for far in range(4)
]


def far_pairs(change):
    return [
        (device(x, y, 2 * far + pair + SHIFT[core], core), device(x, y, 2 * change(far) + pair + SHIFT[core], core))
        for core in range(2) for far in range(4) for pair in range(2) for x in range(4) for y in range(4)
    ]


PEERS = 32
ROWS, D = 128, 2048
HALF = ROWS // 2
WIDE = D // 4
STEPS = 4
ROOM_A = 60 << 20
ROOM_B = 8 << 20
VMEM = 8 << 20
STEP_ROWS = HALF // STEPS
STEP_PEERS = PEERS // STEPS


def spots():
    row, col = lax.axis_index("row"), lax.axis_index("col")
    core = lax.rem(col, 2)
    x, y = col // 8 * 2 + lax.rem(row, 2), lax.rem(col // 2, 4)
    return core, jnp.where(core == 0, x, y), jnp.where(core == 0, y, x)


def chunk_ahead(d, own):
    core, mine, theirs = spots()
    return core * 4 + lax.rem(mine + d, 4) if own else (1 - core) * 4 + lax.rem(theirs + d, 4)


def place_kernel(which, *refs):
    outs, sems = refs[-4:-1], refs[-1]
    copies = []
    for i, (own, d) in enumerate(which):
        at = chunk_ahead(4 - d, own) * 2
        for k in range(3):
            for g in range(4):
                copies.append(
                    pltpu.make_async_copy(
                        refs[i].at[:, g, :, pl.ds(k * WIDE, WIDE)],
                        outs[k].at[pl.ds(at, 2), :, pl.ds(g * WIDE, WIDE)],
                        sems.at[i, k, g],
                    )
                )
    for copy in copies:
        copy.start()
    for copy in copies:
        copy.wait()


def place_chunks(every, which, before):
    anywhere = pl.BlockSpec(memory_space=pl.ANY)
    chunks = [every[name] for name in which]
    n = len(chunks)
    return pl.pallas_call(
        functools.partial(place_kernel, which),
        in_specs=[anywhere] * (n + len(before)),
        out_specs=[anywhere] * 3,
        out_shape=[jax.ShapeDtypeStruct((ROWS // 8, 8, D), jnp.float32)] * 3,
        scratch_shapes=[pltpu.SemaphoreType.DMA((n, 3, 4))],
        input_output_aliases={n + k: k for k in range(len(before))},
        compiler_params=pltpu.CompilerParams(vmem_limit_bytes=8 << 20),
        name="place_chunks",
    )(*(chunk.reshape(2, 4, 8, 3 * WIDE) for chunk in chunks), *before)


def across_cores(x):
    return lax.ppermute(x, AXES, [(i, i ^ 1) for i in range(256)])


def exchange(x, groups):
    return lax.all_to_all(x, AXES, 0, 0, axis_index_groups=groups, tiled=True)


def repeat(x, groups):
    return jnp.broadcast_to(x[None], (len(groups[0]),) + x.shape)


def far_sum(x):
    x = x + lax.ppermute(x, AXES, far_pairs(lambda far: far ^ 1))
    return x + lax.ppermute(x, AXES, far_pairs(lambda far: far ^ 3))


def adam(arrays):
    old, first, second, gradient = (x[0, 0] for x in arrays)
    first = 0.9 * first + 0.1 * gradient
    second = 0.95 * second + 0.05 * gradient * gradient
    scaled = second * (1.0 / bias_two)
    bottom = bias_one * (scaled * lax.rsqrt(scaled)) + bias_one * 1e-08
    return old - 0.003 * (first / bottom + 0.1 * old), first, second


def lay_kernel(*refs):
    for i in range(len(refs) - 3):

        @pl.when(pl.program_id(0) == i)
        def _():
            for k in range(3):
                for p in range(8):
                    value = refs[k][8 * (p // 4) : 8 * (p // 4) + 8, p % 4 * WIDE : (p % 4 + 1) * WIDE]
                    refs[3 + i][p, :, k * WIDE : (k + 1) * WIDE] = value


def lay_chunks(arrays, own):
    chunk = (8, 8, 3 * WIDE)

    def source(i):
        return chunk_ahead(jnp.where(i == 0, WAYS[0], jnp.where(i == 1, WAYS[1], jnp.where(i == 2, WAYS[2], 0))), own), 0

    return pl.pallas_call(
        lay_kernel,
        grid=(4,),
        in_specs=[pl.BlockSpec((16, D), source)] * 3,
        out_specs=[pl.BlockSpec(chunk, lambda i: (0, 0, 0))] * 4,
        out_shape=[jax.ShapeDtypeStruct(chunk, jnp.float32)] * 4,
        compiler_params=pltpu.CompilerParams(vmem_limit_bytes=12 << 20),
        name="lay_chunks",
    )(*arrays)


def on_device(*arrays):
    arrays = adam(arrays)
    received = [across_cores(chunk) for chunk in lay_chunks(arrays, False)]
    sums = [own + theirs for own, theirs in zip(lay_chunks(arrays, True), received)]
    other = [lax.ppermute(chunk, AXES, ring(d)) for chunk, d in zip(sums, WAYS)]
    mine = (sums[3] + other[0]) + (other[1] + other[2])
    mine = jnp.sum(exchange(mine, SECOND), axis=0)
    mine = far_sum(mine) * (1.0 / 256.0)
    mine = exchange(repeat(mine, SECOND), SECOND)
    chunks = {(True, 0): mine}
    chunks.update({(True, d): lax.ppermute(mine, AXES, ring(d)) for d in WAYS})
    chunks.update({(False, d): across_cores(chunks[True, d]) for d in (0,) + WAYS})
    names = [(own, d) for own in (True, False) for d in (0,) + WAYS]
    outs = place_chunks(chunks, names[:SPLIT], ())
    outs = place_chunks(chunks, names[SPLIT:], outs)
    return tuple(out.reshape(ROWS, D) for out in outs)


def solution(mesh):
    spec = P("row", "col", None, None)
    return jax.shard_map(on_device, mesh=mesh, in_specs=(spec,) * 4, out_specs=(P(),) * 3, check_vma=False)
```

```python
import functools

import jax
import jax.numpy as jnp
from jax import lax
from jax.experimental import pallas as pl
from jax.experimental.pallas import tpu as pltpu
from jax.sharding import PartitionSpec as P

bias_one = 0.9999734386011124
bias_two = 0.994079470779666

AXES = ("row", "col")
SHIFT = (0, 0)
WAYS = (2, 1, 3)
BACK = (1, 3, 2)
SPLIT = 6


def device(x, y, z, core):
    return (z % 8 * 2 + x % 2) * 16 + x // 2 * 8 + y * 2 + core


def place(core, along, pair, across, far):
    x, y = (along, across) if core == 0 else (across, along)
    return device(x, y, 2 * far + pair + SHIFT[core], core)


def ring(change):
    return [
        (place(core, along, pair, across, far), place(core, (along + change) % 4, pair, across, far))
        for core in range(2) for along in range(4) for pair in range(2) for across in range(4) for far in range(4)
    ]


SECOND = [
    [place(core, along, pair, across, far) for across in range(4) for pair in range(2)]
    for core in range(2) for along in range(4) for far in range(4)
]


def far_pairs(change):
    return [
        (device(x, y, 2 * far + pair + SHIFT[core], core), device(x, y, 2 * change(far) + pair + SHIFT[core], core))
        for core in range(2) for far in range(4) for pair in range(2) for x in range(4) for y in range(4)
    ]


PEERS = 32
ROWS, D = 128, 2048
HALF = ROWS // 2
WIDE = D // 4
STEPS = 4
ROOM_A = 60 << 20
ROOM_B = 8 << 20
VMEM = 8 << 20
STEP_ROWS = HALF // STEPS
STEP_PEERS = PEERS // STEPS


def spots():
    row, col = lax.axis_index("row"), lax.axis_index("col")
    core = lax.rem(col, 2)
    x, y = col // 8 * 2 + lax.rem(row, 2), lax.rem(col // 2, 4)
    return core, jnp.where(core == 0, x, y), jnp.where(core == 0, y, x)


def chunk_ahead(d, own):
    core, mine, theirs = spots()
    return core * 4 + lax.rem(mine + d, 4) if own else (1 - core) * 4 + lax.rem(theirs + d, 4)


def place_kernel(which, *refs):
    outs, sems = refs[-4:-1], refs[-1]
    copies = []
    for i, (own, d) in enumerate(which):
        at = chunk_ahead(4 - d, own) * 2
        for k in range(3):
            for g in range(4):
                copies.append(
                    pltpu.make_async_copy(
                        refs[i].at[:, g, :, pl.ds(k * WIDE, WIDE)],
                        outs[k].at[pl.ds(at, 2), :, pl.ds(g * WIDE, WIDE)],
                        sems.at[i, k, g],
                    )
                )
    for copy in copies:
        copy.start()
    for copy in copies:
        copy.wait()


def place_chunks(every, which, before):
    anywhere = pl.BlockSpec(memory_space=pl.ANY)
    chunks = [every[name] for name in which]
    n = len(chunks)
    return pl.pallas_call(
        functools.partial(place_kernel, which),
        in_specs=[anywhere] * (n + len(before)),
        out_specs=[anywhere] * 3,
        out_shape=[jax.ShapeDtypeStruct((ROWS // 8, 8, D), jnp.float32)] * 3,
        scratch_shapes=[pltpu.SemaphoreType.DMA((n, 3, 4))],
        input_output_aliases={n + k: k for k in range(len(before))},
        compiler_params=pltpu.CompilerParams(vmem_limit_bytes=8 << 20),
        name="place_chunks",
    )(*(chunk.reshape(2, 4, 8, 3 * WIDE) for chunk in chunks), *before)


def across_cores(x):
    return lax.ppermute(x, AXES, [(i, i ^ 1) for i in range(256)])


def exchange(x, groups):
    return lax.all_to_all(x, AXES, 0, 0, axis_index_groups=groups, tiled=True)


def repeat(x, groups):
    return jnp.broadcast_to(x[None], (len(groups[0]),) + x.shape)


def far_sum(x):
    x = x + lax.ppermute(x, AXES, far_pairs(lambda far: far ^ 1))
    return x + lax.ppermute(x, AXES, far_pairs(lambda far: far ^ 3))


def adam(arrays):
    old, first, second, gradient = (x[0, 0] for x in arrays)
    first = 0.9 * first + 0.1 * gradient
    second = 0.95 * second + 0.05 * gradient * gradient
    scaled = second * (1.0 / bias_two)
    bottom = bias_one * (scaled * lax.rsqrt(scaled)) + bias_one * 1e-08
    return old - 0.003 * (first / bottom + 0.1 * old), first, second


def lay_kernel(*refs):
    for i in range(len(refs) - 3):

        @pl.when(pl.program_id(0) == i)
        def _():
            for k in range(3):
                for p in range(8):
                    value = refs[k][8 * (p // 4) : 8 * (p // 4) + 8, p % 4 * WIDE : (p % 4 + 1) * WIDE]
                    refs[3 + i][p, :, k * WIDE : (k + 1) * WIDE] = value


def lay_chunks(arrays, own):
    chunk = (8, 8, 3 * WIDE)

    def source(i):
        return chunk_ahead(jnp.where(i == 0, WAYS[0], jnp.where(i == 1, WAYS[1], jnp.where(i == 2, WAYS[2], 0))), own), 0

    return pl.pallas_call(
        lay_kernel,
        grid=(4,),
        in_specs=[pl.BlockSpec((16, D), source)] * 3,
        out_specs=[pl.BlockSpec(chunk, lambda i: (0, 0, 0))] * 4,
        out_shape=[jax.ShapeDtypeStruct(chunk, jnp.float32)] * 4,
        compiler_params=pltpu.CompilerParams(vmem_limit_bytes=12 << 20),
        name="lay_chunks",
    )(*arrays)


def on_device(*arrays):
    arrays = adam(arrays)
    received = [across_cores(chunk) for chunk in lay_chunks(arrays, False)]
    sums = [own + theirs for own, theirs in zip(lay_chunks(arrays, True), received)]
    other = [lax.ppermute(chunk, AXES, ring(d)) for chunk, d in zip(sums, WAYS)]
    mine = (sums[3] + other[0]) + (other[1] + other[2])
    mine = jnp.sum(exchange(mine, SECOND), axis=0)
    mine = far_sum(mine) * (1.0 / 256.0)
    mine = exchange(repeat(mine, SECOND), SECOND)
    chunks = {(True, 0): mine}
    chunks.update({(True, d): lax.ppermute(mine, AXES, ring(d)) for d in BACK})
    first, second, last = BACK
    chunks[False, 0], chunks[False, first] = across_cores(mine), across_cores(chunks[True, first])
    outs = place_chunks(chunks, [(True, 0), (True, first)], ())
    chunks[True, second], outs = lax.optimization_barrier((chunks[True, second], outs))
    chunks[False, second], chunks[False, last] = across_cores(chunks[True, second]), across_cores(chunks[True, last])
    outs = place_chunks(chunks, [(True, second), (True, last), (False, 0), (False, first)], outs)
    outs = place_chunks(chunks, [(False, second), (False, last)], outs)
    return tuple(out.reshape(ROWS, D) for out in outs)


def solution(mesh):
    spec = P("row", "col", None, None)
    return jax.shard_map(on_device, mesh=mesh, in_specs=(spec,) * 4, out_specs=(P(),) * 3, check_vma=False)
```

```python
import functools

import jax
import jax.numpy as jnp
from jax import lax
from jax.experimental import pallas as pl
from jax.experimental.pallas import tpu as pltpu
from jax.sharding import PartitionSpec as P

bias_one = 0.9999734386011124
bias_two = 0.994079470779666

AXES = ("row", "col")
SHIFT = (0, 0)
WAYS = (2, 1, 3)
BACK = (1, 3, 2)
SPLIT = 6


def device(x, y, z, core):
    return (z % 8 * 2 + x % 2) * 16 + x // 2 * 8 + y * 2 + core


def place(core, along, pair, across, far):
    x, y = (along, across) if core == 0 else (across, along)
    return device(x, y, 2 * far + pair + SHIFT[core], core)


def ring(change):
    return [
        (place(core, along, pair, across, far), place(core, (along + change) % 4, pair, across, far))
        for core in range(2) for along in range(4) for pair in range(2) for across in range(4) for far in range(4)
    ]


SECOND = [
    [place(core, along, pair, across, far) for pair in range(2) for across in range(4)]
    for core in range(2) for along in range(4) for far in range(4)
]


def far_pairs(change):
    return [
        (device(x, y, 2 * far + pair + SHIFT[core], core), device(x, y, 2 * change(far) + pair + SHIFT[core], core))
        for core in range(2) for far in range(4) for pair in range(2) for x in range(4) for y in range(4)
    ]


PEERS = 32
ROWS, D = 128, 2048
HALF = ROWS // 2
WIDE = D // 4
STEPS = 4
ROOM_A = 60 << 20
ROOM_B = 8 << 20
VMEM = 8 << 20
STEP_ROWS = HALF // STEPS
STEP_PEERS = PEERS // STEPS


def spots():
    row, col = lax.axis_index("row"), lax.axis_index("col")
    core = lax.rem(col, 2)
    x, y = col // 8 * 2 + lax.rem(row, 2), lax.rem(col // 2, 4)
    return core, jnp.where(core == 0, x, y), jnp.where(core == 0, y, x)


def chunk_ahead(d, own):
    core, mine, theirs = spots()
    return core * 4 + lax.rem(mine + d, 4) if own else (1 - core) * 4 + lax.rem(theirs + d, 4)


def place_kernel(which, *refs):
    outs, sems = refs[-4:-1], refs[-1]
    copies = []
    for i, (own, d) in enumerate(which):
        at = chunk_ahead(4 - d, own) * 2
        for k in range(3):
            for g in range(4):
                copies.append(
                    pltpu.make_async_copy(
                        refs[i].at[:, g, :, pl.ds(k * WIDE, WIDE)],
                        outs[k].at[pl.ds(at, 2), :, pl.ds(g * WIDE, WIDE)],
                        sems.at[i, k, g],
                    )
                )
    for copy in copies:
        copy.start()
    for copy in copies:
        copy.wait()


def place_chunks(every, which, before):
    anywhere = pl.BlockSpec(memory_space=pl.ANY)
    chunks = [every[name] for name in which]
    n = len(chunks)
    return pl.pallas_call(
        functools.partial(place_kernel, which),
        in_specs=[anywhere] * (n + len(before)),
        out_specs=[anywhere] * 3,
        out_shape=[jax.ShapeDtypeStruct((ROWS // 8, 8, D), jnp.float32)] * 3,
        scratch_shapes=[pltpu.SemaphoreType.DMA((n, 3, 4))],
        input_output_aliases={n + k: k for k in range(len(before))},
        compiler_params=pltpu.CompilerParams(vmem_limit_bytes=8 << 20),
        name="place_chunks",
    )(*(chunk.reshape(2, 4, 8, 3 * WIDE) for chunk in chunks), *before)


def across_cores(x):
    return lax.ppermute(x, AXES, [(i, i ^ 1) for i in range(256)])


def exchange(x, groups):
    return lax.all_to_all(x, AXES, 0, 0, axis_index_groups=groups, tiled=True)


def repeat(x, groups):
    return jnp.broadcast_to(x[None], (len(groups[0]),) + x.shape)


def far_sum(x):
    x = x + lax.ppermute(x, AXES, far_pairs(lambda far: far ^ 1))
    return x + lax.ppermute(x, AXES, far_pairs(lambda far: far ^ 3))


def adam(arrays):
    old, first, second, gradient = (x[0, 0] for x in arrays)
    first = 0.9 * first + 0.1 * gradient
    second = 0.95 * second + 0.05 * gradient * gradient
    scaled = second * (1.0 / bias_two)
    bottom = bias_one * (scaled * lax.rsqrt(scaled)) + bias_one * 1e-08
    return old - 0.003 * (first / bottom + 0.1 * old), first, second


def lay_kernel(*refs):
    for i in range(len(refs) - 3):

        @pl.when(pl.program_id(0) == i)
        def _():
            for k in range(3):
                for p in range(8):
                    value = refs[k][8 * (p // 4) : 8 * (p // 4) + 8, p % 4 * WIDE : (p % 4 + 1) * WIDE]
                    refs[3 + i][p, :, k * WIDE : (k + 1) * WIDE] = value


def lay_chunks(arrays, own):
    chunk = (8, 8, 3 * WIDE)

    def source(i):
        return chunk_ahead(jnp.where(i == 0, WAYS[0], jnp.where(i == 1, WAYS[1], jnp.where(i == 2, WAYS[2], 0))), own), 0

    return pl.pallas_call(
        lay_kernel,
        grid=(4,),
        in_specs=[pl.BlockSpec((16, D), source)] * 3,
        out_specs=[pl.BlockSpec(chunk, lambda i: (0, 0, 0))] * 4,
        out_shape=[jax.ShapeDtypeStruct(chunk, jnp.float32)] * 4,
        compiler_params=pltpu.CompilerParams(vmem_limit_bytes=12 << 20),
        name="lay_chunks",
    )(*arrays)


def on_device(*arrays):
    arrays = adam(arrays)
    received = [across_cores(chunk) for chunk in lay_chunks(arrays, False)]
    sums = [own + theirs for own, theirs in zip(lay_chunks(arrays, True), received)]
    other = [lax.ppermute(chunk, AXES, ring(d)) for chunk, d in zip(sums, WAYS)]
    mine = (sums[3] + other[0]) + (other[1] + other[2])
    mine = jnp.sum(exchange(mine, SECOND), axis=0)
    mine = far_sum(mine) * (1.0 / 256.0)
    mine = exchange(repeat(mine, SECOND), SECOND)
    chunks = {(True, 0): mine}
    chunks.update({(True, d): lax.ppermute(mine, AXES, ring(d)) for d in BACK})
    first, second, last = BACK
    chunks[False, 0], chunks[False, first] = across_cores(mine), across_cores(chunks[True, first])
    outs = place_chunks(chunks, [(True, 0), (True, first)], ())
    chunks[True, second], outs = lax.optimization_barrier((chunks[True, second], outs))
    chunks[False, second], chunks[False, last] = across_cores(chunks[True, second]), across_cores(chunks[True, last])
    outs = place_chunks(chunks, [(True, second), (True, last), (False, 0), (False, first)], outs)
    outs = place_chunks(chunks, [(False, second), (False, last)], outs)
    return tuple(out.reshape(ROWS, D) for out in outs)


def solution(mesh):
    spec = P("row", "col", None, None)
    return jax.shard_map(on_device, mesh=mesh, in_specs=(spec,) * 4, out_specs=(P(),) * 3, check_vma=False)
```

```python
import functools

import jax
import jax.numpy as jnp
from jax import lax
from jax.experimental import pallas as pl
from jax.experimental.pallas import tpu as pltpu
from jax.sharding import PartitionSpec as P

bias_one = 0.9999734386011124
bias_two = 0.994079470779666

AXES = ("row", "col")
SHIFT = (0, 0)
WAYS = (2, 3, 1)
BACK = (1, 3, 2)
SPLIT = 6


def device(x, y, z, core):
    return (z % 8 * 2 + x % 2) * 16 + x // 2 * 8 + y * 2 + core


def place(core, along, pair, across, far):
    x, y = (along, across) if core == 0 else (across, along)
    return device(x, y, 2 * far + pair + SHIFT[core], core)


def ring(change):
    return [
        (place(core, along, pair, across, far), place(core, (along + change) % 4, pair, across, far))
        for core in range(2) for along in range(4) for pair in range(2) for across in range(4) for far in range(4)
    ]


SECOND = [
    [place(core, along, pair, across, far) for pair in range(2) for across in range(4)]
    for core in range(2) for along in range(4) for far in range(4)
]


def far_pairs(change):
    return [
        (device(x, y, 2 * far + pair + SHIFT[core], core), device(x, y, 2 * change(far) + pair + SHIFT[core], core))
        for core in range(2) for far in range(4) for pair in range(2) for x in range(4) for y in range(4)
    ]


PEERS = 32
ROWS, D = 128, 2048
HALF = ROWS // 2
WIDE = D // 4
STEPS = 4
ROOM_A = 60 << 20
ROOM_B = 8 << 20
VMEM = 8 << 20
STEP_ROWS = HALF // STEPS
STEP_PEERS = PEERS // STEPS


def spots():
    row, col = lax.axis_index("row"), lax.axis_index("col")
    core = lax.rem(col, 2)
    x, y = col // 8 * 2 + lax.rem(row, 2), lax.rem(col // 2, 4)
    return core, jnp.where(core == 0, x, y), jnp.where(core == 0, y, x)


def chunk_ahead(d, own):
    core, mine, theirs = spots()
    return core * 4 + lax.rem(mine + d, 4) if own else (1 - core) * 4 + lax.rem(theirs + d, 4)


def place_kernel(which, *refs):
    outs, sems = refs[-4:-1], refs[-1]
    copies = []
    for i, (own, d) in enumerate(which):
        at = chunk_ahead(4 - d, own) * 2
        for k in range(3):
            for g in range(4):
                copies.append(
                    pltpu.make_async_copy(
                        refs[i].at[:, g, :, pl.ds(k * WIDE, WIDE)],
                        outs[k].at[pl.ds(at, 2), :, pl.ds(g * WIDE, WIDE)],
                        sems.at[i, k, g],
                    )
                )
    for copy in copies:
        copy.start()
    for copy in copies:
        copy.wait()


def place_chunks(every, which, before):
    anywhere = pl.BlockSpec(memory_space=pl.ANY)
    chunks = [every[name] for name in which]
    n = len(chunks)
    return pl.pallas_call(
        functools.partial(place_kernel, which),
        in_specs=[anywhere] * (n + len(before)),
        out_specs=[anywhere] * 3,
        out_shape=[jax.ShapeDtypeStruct((ROWS // 8, 8, D), jnp.float32)] * 3,
        scratch_shapes=[pltpu.SemaphoreType.DMA((n, 3, 4))],
        input_output_aliases={n + k: k for k in range(len(before))},
        compiler_params=pltpu.CompilerParams(vmem_limit_bytes=8 << 20),
        name="place_chunks",
    )(*(chunk.reshape(2, 4, 8, 3 * WIDE) for chunk in chunks), *before)


def across_cores(x):
    return lax.ppermute(x, AXES, [(i, i ^ 1) for i in range(256)])


def exchange(x, groups):
    return lax.all_to_all(x, AXES, 0, 0, axis_index_groups=groups, tiled=True)


def repeat(x, groups):
    return jnp.broadcast_to(x[None], (len(groups[0]),) + x.shape)


def far_sum(x):
    x = x + lax.ppermute(x, AXES, far_pairs(lambda far: far ^ 1))
    return x + lax.ppermute(x, AXES, far_pairs(lambda far: far ^ 3))


def adam(arrays):
    old, first, second, gradient = (x[0, 0] for x in arrays)
    first = 0.9 * first + 0.1 * gradient
    second = 0.95 * second + 0.05 * gradient * gradient
    scaled = second * (1.0 / bias_two)
    bottom = bias_one * (scaled * lax.rsqrt(scaled)) + bias_one * 1e-08
    return old - 0.003 * (first / bottom + 0.1 * old), first, second


def lay_kernel(*refs):
    for i in range(len(refs) - 3):

        @pl.when(pl.program_id(0) == i)
        def _():
            for k in range(3):
                for p in range(8):
                    value = refs[k][8 * (p // 4) : 8 * (p // 4) + 8, p % 4 * WIDE : (p % 4 + 1) * WIDE]
                    refs[3 + i][p, :, k * WIDE : (k + 1) * WIDE] = value


def lay_chunks(arrays, own):
    chunk = (8, 8, 3 * WIDE)

    def source(i):
        return chunk_ahead(jnp.where(i == 0, WAYS[0], jnp.where(i == 1, WAYS[1], jnp.where(i == 2, WAYS[2], 0))), own), 0

    return pl.pallas_call(
        lay_kernel,
        grid=(4,),
        in_specs=[pl.BlockSpec((16, D), source)] * 3,
        out_specs=[pl.BlockSpec(chunk, lambda i: (0, 0, 0))] * 4,
        out_shape=[jax.ShapeDtypeStruct(chunk, jnp.float32)] * 4,
        compiler_params=pltpu.CompilerParams(vmem_limit_bytes=12 << 20),
        name="lay_chunks",
    )(*arrays)


def on_device(*arrays):
    arrays = adam(arrays)
    received = [across_cores(chunk) for chunk in lay_chunks(arrays, False)]
    sums = [own + theirs for own, theirs in zip(lay_chunks(arrays, True), received)]
    other = [lax.ppermute(chunk, AXES, ring(d)) for chunk, d in zip(sums, WAYS)]
    mine = (sums[3] + other[0]) + (other[1] + other[2])
    mine = jnp.sum(exchange(mine, SECOND), axis=0)
    mine = far_sum(mine) * (1.0 / 256.0)
    mine = exchange(repeat(mine, SECOND), SECOND)
    chunks = {(True, 0): mine}
    chunks.update({(True, d): lax.ppermute(mine, AXES, ring(d)) for d in BACK})
    first, second, last = BACK
    chunks[False, 0], chunks[False, first] = across_cores(mine), across_cores(chunks[True, first])
    outs = place_chunks(chunks, [(True, 0), (True, first)], ())
    chunks[True, second], outs = lax.optimization_barrier((chunks[True, second], outs))
    chunks[False, second], chunks[False, last] = across_cores(chunks[True, second]), across_cores(chunks[True, last])
    outs = place_chunks(chunks, [(True, second), (True, last), (False, 0), (False, first)], outs)
    outs = place_chunks(chunks, [(False, second), (False, last)], outs)
    return tuple(out.reshape(ROWS, D) for out in outs)


def solution(mesh):
    spec = P("row", "col", None, None)
    return jax.shard_map(on_device, mesh=mesh, in_specs=(spec,) * 4, out_specs=(P(),) * 3, check_vma=False)
```
